128 devices in a mesh: row: 16 (over y, x), col: 8 (over z, core).
Axes of the slice: x: 4, y: 4, z: 4, core: 2. Of those that a mesh axis runs over, the one named last changes fastest.
Arguments:
- p_cov: bfloat16 [8192, 8192], P('row', 'col'), may hold values from -6 to 6, as said below
- f_blocks: bfloat16 [64, 7, 128, 128], P('row'), may hold values from -0.1875 to 0.1875
- stencil_cols: int32 [64, 7], replicated, may hold values from 0 to 63, as said below
- localization_weights: bfloat16 [8192, 8192], P('row', 'col'), may hold values from 0.25 to 1, as said below
- block_mask: int32 [64, 64], P('row', 'col'), may hold values from 0 to 1, as said below
- disturbance_variances: float32 [8192], P('row'), may hold values from 0.5 to 2
Outputs:
- predicted_spread_matrix: float32 [8192, 8192], P('row', 'col')
The draws below stay inside these ranges and needn't reach their ends.
Inputs may be any that keep to these rules, and one draw needn't show every extreme that they name: `stencil_cols`: block row i lists i, i - 1, i + 1, one block 2 to 3 above and one below, and i - 4 and i + 4, each clamped to 0 .. 63. Symmetric: p_cov equals its transpose. `localization_weights`: Symmetric: taper equals its transpose. Symmetric: block_mask equals its transpose.
All inputs are finite; a program needn't handle non-finite values.
Results may differ from the reference program's by a relative error of at most 0.0029.
Values may be sent and summed in bfloat16 or wider, within the bound.
A program may use at most 64 MiB of HBM per device.

```python
import math
import jax
import jax.numpy as jnp

BS = 128
STENCIL = 7
BAND = 4
NB = 64
STATE_DIMENSION = 8192


def draw_stencil_cols(key, part):
    first_key, second_key = jax.random.split(jax.random.fold_in(key, 17))
    base = jnp.arange(NB, dtype=jnp.int32)
    upper = jax.random.randint(first_key, (NB,), 2, BAND, dtype=jnp.int32)
    lower = jax.random.randint(second_key, (NB,), 2, BAND, dtype=jnp.int32)
    zeros = jnp.zeros((NB,), jnp.int32)
    ones = jnp.ones((NB,), jnp.int32)
    reach = jnp.full((NB,), BAND, jnp.int32)
    offsets = jnp.stack([zeros, ones, -ones, upper, -lower, reach, -reach], axis=1)
    return jnp.clip(base[:, None] + offsets, 0, NB - 1).astype(jnp.int32)


def draw_p_cov(key, part):
    first_key = jax.random.fold_in(jax.random.fold_in(key, 29), 0)
    raw = jax.random.normal(first_key, (STATE_DIMENSION, STATE_DIMENSION), jnp.float32)
    sym = (raw + raw.T) * 0.70710678
    return jnp.clip(sym, -6.0, 6.0).astype(jnp.bfloat16)


def draw_localization_weights(key, part):
    raw = jax.random.uniform(jax.random.fold_in(key, 31), (STATE_DIMENSION, STATE_DIMENSION), jnp.float32, 0.0, 1.0)
    values = 0.25 + 0.75 * raw
    lower = jnp.tril(values)
    sym = lower + jnp.tril(values, -1).T
    return sym.astype(jnp.bfloat16)


def draw_block_mask(key, part):
    raw = jax.random.randint(jax.random.fold_in(key, 37), (NB, NB), 0, 4, dtype=jnp.int32)
    kept = (raw > 0).astype(jnp.int32)
    lower = jnp.tril(kept)
    return (lower + jnp.tril(kept, -1).T).astype(jnp.int32)


def shard_levels(key, dims, pieces, low, largest):
    def one(axis_at, shards_of):
        heights = jax.random.uniform(jax.random.fold_in(jax.random.fold_in(key, 6), axis_at), (shards_of,), jnp.float32, low / len(pieces), largest / len(pieces))
        return jnp.repeat(jnp.exp(heights), dims[axis_at] // shards_of).reshape((-1,) + (1,) * (len(dims) - axis_at - 1))

    loudness = one(*pieces[0])
    for cut in pieces[1:]:
        loudness = loudness * one(*cut)
    return loudness


def scatter_about(stream_key, extent, width, most, shards=(), kind=jnp.bfloat16):
    values = jax.random.normal(stream_key, extent, jnp.float32) * width
    if len(shards) > 0:
        values = shard_levels(stream_key, extent, shards, -0.22, 0.18) * values
    return jnp.clip(values, min=-most, max=most).astype(kind)


def setup_inputs(seed: int = 0) -> dict:
    streams_of = jax.random.split(jax.random.key(seed), 7)
    p_cov = draw_p_cov(jax.random.fold_in(streams_of[6], 71), 0)
    f_blocks = scatter_about(streams_of[1], (NB, STENCIL, BS, BS), (STENCIL * BS) ** -0.5, 0.1875, ((0, 16),))
    stencil_cols = draw_stencil_cols(jax.random.fold_in(streams_of[6], 71), 0)
    localization_weights = draw_localization_weights(jax.random.fold_in(streams_of[6], 71), 0)
    block_mask = draw_block_mask(jax.random.fold_in(streams_of[6], 71), 0)
    disturbance_variances = jnp.clip(jnp.exp(math.log(2.0) - 1.3862944 * jax.random.uniform(streams_of[5], (STATE_DIMENSION,), jnp.float32) ** shard_levels(streams_of[5], (STATE_DIMENSION,), ((0, 16),), -0.2, 0.2)), 0.5, 2.0)
    return {"p_cov": p_cov, "f_blocks": f_blocks, "stencil_cols": stencil_cols, "localization_weights": localization_weights, "block_mask": block_mask, "disturbance_variances": disturbance_variances}


def reference(p_cov, f_blocks, stencil_cols, localization_weights, block_mask, disturbance_variances):
    covariance_rows = p_cov.reshape(NB, BS, STATE_DIMENSION)
    inter = jnp.zeros((NB, BS, STATE_DIMENSION), jnp.float32)
    for entry in range(STENCIL):
        picked = covariance_rows[stencil_cols[:, entry]].astype(jnp.float32)
        inter = inter + jnp.einsum("iab,ibn->ian", f_blocks[:, entry].astype(jnp.float32), picked)
    inter = inter.reshape(STATE_DIMENSION, STATE_DIMENSION).astype(jnp.bfloat16)
    inter_cols = inter.reshape(STATE_DIMENSION, NB, BS)
    spread = jnp.zeros((STATE_DIMENSION, NB, BS), jnp.float32)
    for entry in range(STENCIL):
        picked = inter_cols[:, stencil_cols[:, entry], :].astype(jnp.float32)
        spread = spread + jnp.einsum("rjb,jab->rja", picked, f_blocks[:, entry].astype(jnp.float32))
    filtered_tile_entries = spread.reshape(NB, BS, NB, BS) * block_mask.astype(jnp.float32)[:, None, :, None]
    predicted_spread_matrix = localization_weights.astype(jnp.float32) * filtered_tile_entries.reshape(STATE_DIMENSION, STATE_DIMENSION)
    main_slot_position = jnp.arange(STATE_DIMENSION, dtype=jnp.int32)
    return predicted_spread_matrix.at[main_slot_position, main_slot_position].add(disturbance_variances)
```

```python
import jax
import jax.numpy as jnp
from jax import lax
from jax.experimental import pallas as pl
from jax.experimental.pallas import tpu as pltpu
from jax.sharding import PartitionSpec as P

MESH = pl.DeviceIdType.MESH
E7 = 7
BS = 128
CW = 256
NT = (((1,), (1,)), ((), ()))


def remote(src, dst, send, recv, to):
    return pltpu.make_async_remote_copy(src, dst, send, recv, device_id=to, device_id_type=MESH)


def densify(get, rel, put):
    weight = [
        [jnp.where(rel[e] == k, 1.0, 0.0).astype(jnp.float32) for e in range(E7)]
        for k in range(10)
    ]

    def strip(i, carry):
        rows = pl.ds(pl.multiple_of(i * 32, 32), 32)
        blocks = [get(e, rows).astype(jnp.float32) for e in range(E7)]
        for k in range(10):
            total = blocks[0] * weight[k][0]
            for e in range(1, E7):
                total = total + blocks[e] * weight[k][e]
            put(i * 32, k, total.astype(jnp.bfloat16))
        return carry

    lax.fori_loop(0, BS // 32, strip, 0)


def kernel(
    p, f, cols, taper, mask, noise, out,
    pown, up, dn, inter, fown, fbuf, drow, dcol, tap, stage,
    hs, hr, zs, zr, s1, r1, s2, r2, s3, r3, lp, lf, lt, lo,
):
    r, c = lax.axis_index("row"), lax.axis_index("col")
    x, y, z, k = r % 4, r // 4, c // 2, c % 2

    def dev(x, y, z, k):
        return (y * 4 + x, z * 2 + k)

    def chunk(s):
        return s + k * (3 - 2 * s)

    def lanes(ch):
        return pl.ds(pl.multiple_of(ch * CW, CW), CW)

    nxt, prv = ((r + 1) % 16, c), ((r + 15) % 16, c)
    zn, zp = (r, (c + 1) % 8), (r, (c + 7) % 8)
    X = [dev((x + d) % 4, y, z, k) for d in range(4)]
    Y = [dev(x, (y + d) % 4, z, k) for d in range(4)]

    load_f = pltpu.make_async_copy(f, fown, lf.at[0])
    load_p = [pltpu.make_async_copy(p.at[:, lanes(chunk(s))], pown.at[s], lp.at[s]) for s in range(4)]
    load_t = [pltpu.make_async_copy(taper.at[:, lanes(chunk(s))], tap.at[s], lt.at[s]) for s in range(4)]
    load_f.start()
    for s in range(4):
        load_p[s].start()

    barrier = pltpu.get_barrier_semaphore()
    partners = [nxt, prv, zn, zp] + X[1:] + Y[1:]
    for t in partners:
        pl.semaphore_signal(barrier, inc=1, device_id=t, device_id_type=MESH)
    pl.semaphore_wait(barrier, len(partners))

    source = x // 2 == k
    root = (y == z) & source
    h = x % 2
    scatter = [None] + [
        remote(f.at[(y + d) % 4], fbuf.at[(y + d) % 4, h], s1.at[d], r1.at[0], Y[d]) for d in (1, 2, 3)
    ]
    along_x = [None] + [
        remote(fbuf.at[y, h], fbuf.at[y, h], s2.at[d], r2.at[h], X[d]) for d in (1, 2, 3)
    ]
    along_y = [None] + [remote(fbuf.at[y], fbuf.at[y], s3.at[d], r3.at[d], Y[d]) for d in (1, 2, 3)]
    halo = []
    for s in range(4):
        piece = p.at[:, lanes(chunk(s))]
        halo.append((
            remote(piece, up.at[s], hs.at[0, s], hr.at[0, s], nxt),
            remote(piece, dn.at[s], hs.at[1, s], hr.at[1, s], prv),
        ))

    @pl.when(root)
    def _():
        for d in (1, 3, 2):
            scatter[d].start()
        own = pltpu.make_async_copy(f.at[y], fbuf.at[y, h], lf.at[1])
        own.start()
        own.wait()

    for cp in halo[0]:
        cp.start()
    for s in range(4):
        load_t[s].start()

    load_f.wait()

    def own_row(i, carry):
        pair, u = i // 2, i % 2
        base = r * 4 + 2 * pair - 4
        rel = [cols[r * 4 + i, e] - base for e in range(E7)]

        def put(row, kk, block):
            rows = pl.ds(pl.multiple_of(u * BS + row, 32), 32)
            drow[pair, rows, kk * BS:(kk + 1) * BS] = block

        densify(lambda e, rows: fown[i, e, rows, :], rel, put)
        return carry

    lax.fori_loop(0, 4, own_row, 0)

    @pl.when(source & (y != z))
    def _():
        scatter[1].wait_recv()

    @pl.when(source)
    def _():
        for d in (1, 3, 2):
            along_x[d].start()

    for s in (1, 2, 3):
        for cp in halo[s]:
            cp.start()

    for g in (0, 1):
        @pl.when(x != 2 * k + g)
        def _():
            remote(fbuf.at[y, g], fbuf.at[y, g], s2.at[1], r2.at[g], X[1]).wait_recv()
    for d in (1, 3, 2):
        along_y[d].start()

    def col_rows(q):
        def one(g, carry):
            pair, u = 2 * g + q // 2, q % 2
            base = c * 8 + 2 * pair - 4
            rel = [cols[c * 8 + 4 * g + q, e] - base for e in range(E7)]

            def put(row, kk, block):
                rows = pl.ds(pl.multiple_of(u * BS + row, 32), 32)
                dcol[pair, rows, kk * BS:(kk + 1) * BS] = block

            densify(lambda e, rows: fbuf[q, g, e, rows, :], rel, put)
            return carry

        lax.fori_loop(0, 2, one, 0)

    def first_product(s):
        for cp in halo[s]:
            cp.wait_recv()
        load_p[s].wait()
        ch = chunk(s)
        mid = pown[s]
        top = jnp.dot(drow[0, :, 0:512], up[s], preferred_element_type=jnp.float32)
        top += jnp.dot(drow[0, :, 512:1024], mid, preferred_element_type=jnp.float32)
        top += jnp.dot(drow[0, :, 1024:1280], dn[s, 0:256], preferred_element_type=jnp.float32)
        inter[ch + 2, 0:256] = top.astype(jnp.bfloat16)
        low = jnp.dot(drow[1, :, 0:256], up[s, 256:512], preferred_element_type=jnp.float32)
        low += jnp.dot(drow[1, :, 256:768], mid, preferred_element_type=jnp.float32)
        low += jnp.dot(drow[1, :, 768:1280], dn[s], preferred_element_type=jnp.float32)
        inter[ch + 2, 256:512] = low.astype(jnp.bfloat16)

        @pl.when(ch < 2)
        def _():
            remote(inter.at[ch + 2], inter.at[ch + 6], zs.at[s], zr.at[ch + 2], zp).start()

        @pl.when(ch >= 2)
        def _():
            remote(inter.at[ch + 2], inter.at[ch - 2], zs.at[s], zr.at[ch - 2], zn).start()

    first_product(0)
    col_rows(y)
    first_product(1)
    along_y[1].wait_recv()
    col_rows((y + 3) % 4)
    along_y[3].wait_recv()
    col_rows((y + 1) % 4)
    first_product(2)
    first_product(3)
    along_y[2].wait_recv()
    col_rows((y + 2) % 4)

    for i, slot in enumerate((0, 1, 6, 7)):
        remote(inter.at[2], inter.at[slot], zs.at[0], zr.at[i], zn).wait_recv()

    store = []
    for s in range(4):
        ch = chunk(s)
        wide = jnp.concatenate([inter[ch + t] for t in range(5)], axis=1)
        spread = lax.dot_general(wide, dcol[ch], NT, preferred_element_type=jnp.float32)
        load_t[s].wait()
        lane = lax.broadcasted_iota(jnp.int32, (1, CW), 1)
        for u in range(4):
            rows = slice(u * BS, (u + 1) * BS)
            keep = jnp.where(
                lane < BS,
                mask[u, 2 * ch].astype(jnp.float32),
                mask[u, 2 * ch + 1].astype(jnp.float32),
            )
            stage[s, rows, :] = spread[rows] * (tap[s, rows, :].astype(jnp.float32) * keep)
        for t in range(2):
            u = c * 8 + 2 * ch + t - r * 4

            @pl.when((u >= 0) & (u < 4))
            def _():
                eye = lax.broadcasted_iota(jnp.int32, (BS, BS), 0) == lax.broadcasted_iota(
                    jnp.int32, (BS, BS), 1
                )
                rows = pl.ds(pl.multiple_of(u * BS, BS), BS)
                here = (s, rows, slice(t * BS, (t + 1) * BS))
                stage[here] = stage[here] + jnp.where(eye, noise[pl.ds(u, 1), :], 0.0)

        cp = pltpu.make_async_copy(stage.at[s], out.at[:, lanes(ch)], lo.at[s])
        cp.start()
        store.append(cp)
    for cp in store:
        cp.wait()

    for s in range(4):
        for cp in halo[s]:
            cp.wait_send()
        remote(inter.at[2], inter.at[0], zs.at[s], zr.at[0], zn).wait_send()
    for d in (1, 3, 2):
        along_y[d].wait_send()

    @pl.when(root)
    def _():
        for d in (1, 3, 2):
            scatter[d].wait_send()

    @pl.when(source)
    def _():
        for d in (1, 3, 2):
            along_x[d].wait_send()


def on_device(p_cov, f_blocks, stencil_cols, localization_weights, block_mask, disturbance_variances):
    noise = disturbance_variances.reshape(4, BS)
    bf = jnp.bfloat16
    dma = pltpu.SemaphoreType.DMA
    hbm = pl.BlockSpec(memory_space=pl.ANY)
    smem = pl.BlockSpec(memory_space=pltpu.SMEM)
    return pl.pallas_call(
        kernel,
        out_shape=jax.ShapeDtypeStruct((512, 1024), jnp.float32),
        in_specs=[hbm, hbm, smem, hbm, smem, pl.BlockSpec(memory_space=pltpu.VMEM)],
        out_specs=hbm,
        scratch_shapes=[
            pltpu.VMEM((4, 512, CW), bf),
            pltpu.VMEM((4, 512, CW), bf),
            pltpu.VMEM((4, 512, CW), bf),
            pltpu.VMEM((8, 512, CW), bf),
            pltpu.VMEM((4, E7, BS, BS), bf),
            pltpu.VMEM((4, 2, E7, BS, BS), bf),
            pltpu.VMEM((2, 256, 1280), bf),
            pltpu.VMEM((4, 256, 1280), bf),
            pltpu.VMEM((4, 512, CW), bf),
            pltpu.VMEM((4, 512, CW), jnp.float32),
            dma((2, 4)), dma((2, 4)), dma((4,)), dma((4,)),
            dma((4,)), dma((1,)), dma((4,)), dma((2,)), dma((4,)), dma((4,)),
            dma((4,)), dma((2,)), dma((4,)), dma((4,)),
        ],
        compiler_params=pltpu.CompilerParams(
            collective_id=0, has_side_effects=True, vmem_limit_bytes=60 * 2**20
        ),
    )(p_cov, f_blocks, stencil_cols, localization_weights, block_mask, noise)


def solution(mesh):
    placed = (
        P("row", "col"),
        P("row", None, None, None),
        P(),
        P("row", "col"),
        P("row", "col"),
        P("row"),
    )
    return jax.shard_map(
        on_device, mesh=mesh, in_specs=placed, out_specs=P("row", "col"), check_vma=False
    )
```

```python
import jax
import jax.numpy as jnp
from jax import lax
from jax.experimental import pallas as pl
from jax.experimental.pallas import tpu as pltpu
from jax.sharding import PartitionSpec as P

MESH = pl.DeviceIdType.MESH
VMEM_MB = 60
E7 = 7
BS = 128
CW = 256
PART = (pl.ds(0, 2), pl.ds(2, 2), pl.ds(4, 3))
U = range(3)
NT = (((1,), (1,)), ((), ()))


def remote(src, dst, send, recv, to):
    return pltpu.make_async_remote_copy(src, dst, send, recv, device_id=to, device_id_type=MESH)


def densify(get, rel, edge, put):
    weight = [jnp.where(rel[e] == edge, 1.0, 0.0).astype(jnp.float32) for e in range(E7)]

    def strip(i, carry):
        rows = pl.ds(pl.multiple_of(i * 64, 64), 64)
        blocks = [get(e, rows) for e in range(E7)]
        shared = blocks[0].astype(jnp.float32) * weight[0]
        for e in range(1, E7):
            shared = shared + blocks[e].astype(jnp.float32) * weight[e]
        shared = shared.astype(jnp.bfloat16)
        for k in range(10):
            block = jnp.where(edge == k, shared, jnp.zeros_like(shared))
            for e in range(E7):
                block = jnp.where((rel[e] == k) & (edge != k), blocks[e], block)
            put(i * 64, k, block)
        return carry

    lax.fori_loop(0, BS // 64, strip, 0)


def kernel(
    p, f, cols, taper, mask, noise, out,
    pown, up, dn, inter, fown, fbuf, drow, dcol, tap,
    hs, hr, zs, zr, s1, r1, s2, r2, s3, r3, lp, lf, lt,
):
    r, c = lax.axis_index("row"), lax.axis_index("col")
    x, y, z, k = r % 4, r // 4, c // 2, c % 2

    def dev(x, y, z, k):
        return (y * 4 + x, z * 2 + k)

    def chunk(s):
        return s + k * (3 - 2 * s)

    def lanes(ch):
        return pl.ds(pl.multiple_of(ch * CW, CW), CW)

    nxt, prv = ((r + 1) % 16, c), ((r + 15) % 16, c)
    zn, zp = (r, (c + 1) % 8), (r, (c + 7) % 8)
    X = [dev((x + d) % 4, y, z, k) for d in range(4)]
    Y = [dev(x, (y + d) % 4, z, k) for d in range(4)]

    load_f = pltpu.make_async_copy(f, fown, lf.at[0])
    load_p = [pltpu.make_async_copy(p.at[:, lanes(chunk(s))], pown.at[s], lp.at[s]) for s in range(4)]
    load_t = pltpu.make_async_copy(taper, tap, lt.at[0])
    load_f.start()
    for s in range(4):
        load_p[s].start()

    barrier = pltpu.get_barrier_semaphore()
    partners = [nxt, prv, zn, zp] + X[1:] + Y[1:]
    for t in partners:
        pl.semaphore_signal(barrier, inc=1, device_id=t, device_id_type=MESH)
    pl.semaphore_wait(barrier, len(partners))

    source = x // 2 == k
    root = (y == z) & source
    h = x % 2

    def scatter(d, u):
        q = (y + d) % 4
        return remote(f.at[q, PART[u]], fbuf.at[q, h, PART[u]], s1.at[d, u], r1.at[u], Y[d])

    def along_x(d, g, u):
        here = fbuf.at[y, g, PART[u]]
        return remote(here, here, s2.at[d, u], r2.at[g, u], X[d])

    def along_y(d, g, u, to):
        here = fbuf.at[(y + 4 - d) % 4, g, PART[u]]
        there = (d + to) % 4
        return remote(here, here, s3.at[there, g, u], r3.at[there, g, u], Y[to % 4])

    def from_y(d, g, u):
        here = fbuf.at[(y + 4 - d) % 4, g, PART[u]]
        return remote(here, here, s3.at[0, 0, u], r3.at[d, g, u], Y[1])

    halo = []
    for s in range(4):
        piece = p.at[:, lanes(chunk(s))]
        halo.append((
            remote(piece, up.at[s], hs.at[0, s], hr.at[0, s], nxt),
            remote(piece, dn.at[s], hs.at[1, s], hr.at[1, s], prv),
        ))

    @pl.when(root)
    def _():
        for u in U:
            for d in (2, 1, 3):
                scatter(d, u).start()
        own = pltpu.make_async_copy(f.at[y], fbuf.at[y, h], lf.at[1])
        own.start()
        own.wait()

    for cp in halo[0]:
        cp.start()

    load_f.wait()

    def own_row(i, carry):
        pair, v = i // 2, i % 2
        base = r * 4 + 2 * pair - 4
        rel = [cols[e, r * 4 + i] - base for e in range(E7)]

        def put(row, kk, block):
            rows = pl.ds(pl.multiple_of(v * BS + row, 64), 64)
            drow[pair, rows, kk * BS:(kk + 1) * BS] = block

        densify(lambda e, rows: fown[i, e, rows, :], rel, jnp.where(r < 8, 0, 63) - base, put)
        return carry

    lax.fori_loop(0, 4, own_row, 0)

    kinds = (x == 0, -1), (x == 3, 1)
    plain = (x == 1) | (x == 2)

    def send_y(g, u):
        @pl.when(plain)
        def _():
            for to in (1, -1):
                along_y(0, g, u, to).start()

        for cond, to in kinds:
            @pl.when(cond)
            def _():
                along_y(0, g, u, to).start()
                if g == 0:
                    along_y(0, g, u, -to).start()

    for u in U:
        @pl.when(source & (y != z))
        def _():
            scatter(1, u).wait_recv()

        @pl.when(source)
        def _():
            for d in (2, 1, 3):
                along_x(d, h, u).start()

        for g in (0, 1):
            @pl.when(x == 2 * k + g)
            def _():
                send_y(g, u)

    for u in U:
        for g in (0, 1):
            @pl.when(x != 2 * k + g)
            def _():
                along_x(1, g, u).wait_recv()
                send_y(g, u)

    for s in (1, 2, 3):
        for cp in halo[s]:
            cp.start()
    load_t.start()

    def col_rows(d, groups=(0, 2)):
        q = (y + 4 - d) % 4

        def one(g, carry):
            pair, v = 2 * g + q // 2, q % 2
            base = c * 8 + 2 * pair - 4
            rel = [cols[e, c * 8 + 4 * g + q] - base for e in range(E7)]

            def put(row, kk, block):
                rows = pl.ds(pl.multiple_of(v * BS + row, 64), 64)
                dcol[pair, rows, kk * BS:(kk + 1) * BS] = block

            densify(lambda e, rows: fbuf[q, g, e, rows, :], rel, jnp.where(c < 4, 0, 63) - base, put)
            return carry

        lax.fori_loop(*groups, one, 0)

    def first_product(s):
        for cp in halo[s]:
            cp.wait_recv()
        load_p[s].wait()
        ch = chunk(s)
        mid = pown[s]
        top = jnp.dot(drow[0, :, 0:512], up[s], preferred_element_type=jnp.float32)
        top += jnp.dot(drow[0, :, 512:1024], mid, preferred_element_type=jnp.float32)
        top += jnp.dot(drow[0, :, 1024:1280], dn[s, 0:256], preferred_element_type=jnp.float32)
        inter[ch + 2, 0:256] = top.astype(jnp.bfloat16)
        low = jnp.dot(drow[1, :, 0:256], up[s, 256:512], preferred_element_type=jnp.float32)
        low += jnp.dot(drow[1, :, 256:768], mid, preferred_element_type=jnp.float32)
        low += jnp.dot(drow[1, :, 768:1280], dn[s], preferred_element_type=jnp.float32)
        inter[ch + 2, 256:512] = low.astype(jnp.bfloat16)

        @pl.when(ch < 2)
        def _():
            remote(inter.at[ch + 2], inter.at[ch + 6], zs.at[s], zr.at[ch + 2], zp).start()

        @pl.when(ch >= 2)
        def _():
            remote(inter.at[ch + 2], inter.at[ch - 2], zs.at[s], zr.at[ch - 2], zn).start()

    first_product(0)
    col_rows(0)

    @pl.when(plain)
    def _():
        for u in U:
            from_y(1, 0, u).wait_recv()
            along_y(1, 0, u, 1).start()
            from_y(3, 1, u).wait_recv()
            along_y(3, 1, u, -1).start()

    for cond, to in kinds:
        @pl.when(cond)
        def _():
            for u in U:
                for g in (1, 0):
                    from_y(to % 4, g, u).wait_recv()
                    along_y(to % 4, g, u, to).start()

    first_product(1)

    @pl.when(plain)
    def _():
        for u in U:
            from_y(1, 1, u).wait_recv()

    first = jnp.where(x == 0, 3, 1)
    second = jnp.where(plain, 3, 2)
    third = jnp.where(plain, 2, jnp.where(x == 0, 1, 3))
    col_rows(first)

    for cond, to in kinds:
        @pl.when(cond)
        def _():
            for u in U:
                from_y(2, 1, u).wait_recv()
                along_y(2, 1, u, to).start()

    first_product(2)
    for u in U:
        from_y(second, 0, u).wait_recv()
    col_rows(second)
    first_product(3)

    for i, slot in enumerate((0, 1, 6, 7)):
        remote(inter.at[2], inter.at[slot], zs.at[0], zr.at[i], zn).wait_recv()
    load_t.wait()

    def second_product(ch):
        wide = jnp.concatenate([inter[ch + t] for t in range(5)], axis=1)
        spread = lax.dot_general(wide, dcol[ch], NT, preferred_element_type=jnp.float32)
        lane = lax.broadcasted_iota(jnp.int32, (1, CW), 1)
        for v in range(4):
            rows = slice(v * BS, (v + 1) * BS)
            keep = jnp.where(
                lane < BS,
                mask[v, 2 * ch].astype(jnp.float32),
                mask[v, 2 * ch + 1].astype(jnp.float32),
            )
            out[rows, lanes(ch)] = spread[rows] * (tap[rows, lanes(ch)].astype(jnp.float32) * keep)
        for t in range(2):
            v = c * 8 + 2 * ch + t - r * 4

            @pl.when((v >= 0) & (v < 4))
            def _():
                eye = lax.broadcasted_iota(jnp.int32, (BS, BS), 0) == lax.broadcasted_iota(
                    jnp.int32, (BS, BS), 1
                )
                here = (
                    pl.ds(pl.multiple_of(v * BS, BS), BS),
                    pl.ds(pl.multiple_of(ch * CW + t * BS, BS), BS),
                )
                out[here] = out[here] + jnp.where(eye, noise[pl.ds(v, 1), :], 0.0)

    late = ((y + 4 - third) % 4) // 2
    second_product(1 - late)
    second_product(3 - late)
    for g in (0, 1):
        for u in U:
            from_y(third, g, u).wait_recv()
        col_rows(third, (g, g + 1))
        second_product(2 * g + late)

    for s in range(4):
        for cp in halo[s]:
            cp.wait_send()
        remote(inter.at[2], inter.at[0], zs.at[s], zr.at[0], zn).wait_send()
    for u in U:
        for g in (0, 1):
            for d in (1, 2, 3):
                here = fbuf.at[0, 0, PART[u]]
                remote(here, here, s3.at[d, g, u], r3.at[d, g, u], Y[1]).wait_send()

        @pl.when(root)
        def _():
            for d in (1, 2, 3):
                scatter(d, u).wait_send()

        @pl.when(source)
        def _():
            for d in (1, 2, 3):
                along_x(d, h, u).wait_send()


def on_device(p_cov, f_blocks, stencil_cols, localization_weights, block_mask, disturbance_variances):
    noise = disturbance_variances.reshape(4, BS)
    bf = jnp.bfloat16
    dma = pltpu.SemaphoreType.DMA
    hbm = pl.BlockSpec(memory_space=pltpu.HBM)
    vmem = pl.BlockSpec(memory_space=pltpu.VMEM)
    smem = pl.BlockSpec(memory_space=pltpu.SMEM)
    return pl.pallas_call(
        kernel,
        out_shape=pltpu.VMEM((512, 1024), jnp.float32),
        in_specs=[hbm, hbm, smem, hbm, smem, vmem],
        out_specs=vmem,
        scratch_shapes=[
            pltpu.VMEM((4, 512, CW), bf),
            pltpu.VMEM((4, 512, CW), bf),
            pltpu.VMEM((4, 512, CW), bf),
            pltpu.VMEM((8, 512, CW), bf),
            pltpu.VMEM((4, E7, BS, BS), bf),
            pltpu.VMEM((4, 2, E7, BS, BS), bf),
            pltpu.VMEM((2, 256, 1280), bf),
            pltpu.VMEM((4, 256, 1280), bf),
            pltpu.VMEM((512, 1024), bf),
            dma((2, 4)), dma((2, 4)), dma((4,)), dma((4,)),
            dma((4, 3)), dma((3,)), dma((4, 3)), dma((2, 3)), dma((4, 2, 3)), dma((4, 2, 3)),
            dma((4,)), dma((2,)), dma((1,)),
        ],
        compiler_params=pltpu.CompilerParams(
            collective_id=0, has_side_effects=True, vmem_limit_bytes=VMEM_MB * 2**20
        ),
    )(p_cov, f_blocks, stencil_cols.T, localization_weights, block_mask, noise)

def solution(mesh):
    placed = (
        P("row", "col"),
        P("row", None, None, None),
        P(),
        P("row", "col"),
        P("row", "col"),
        P("row"),
    )
    return jax.shard_map(
        on_device, mesh=mesh, in_specs=placed, out_specs=P("row", "col"), check_vma=False
    )
```

```python
import jax
import jax.numpy as jnp
from jax import lax
from jax.experimental import pallas as pl
from jax.experimental.pallas import tpu as pltpu
from jax.sharding import PartitionSpec as P

MESH = pl.DeviceIdType.MESH
VMEM_MB = 60
E7 = 7
BS = 128
CW = 256
PART = (pl.ds(0, 2), pl.ds(2, 2), pl.ds(4, 3))
U = range(3)
READY = (0, 1, 2, 3, 4), (1, 2, 3, 4), (2, 3, 4), (3, 4, 7)
LAST = (), (5,), (5, 6), (5, 6)
NT = (((1,), (1,)), ((), ()))


def remote(src, dst, send, recv, to):
    return pltpu.make_async_remote_copy(src, dst, send, recv, device_id=to, device_id_type=MESH)


class Between:
    def __init__(self, copy, sends, takes):
        self.copy, self.sends, self.takes = copy, sends, takes

    def start(self):
        pl.when(self.sends)(lambda: self.copy.start())

    def wait_send(self):
        pl.when(self.sends)(lambda: self.copy.wait_send())

    def wait_recv(self):
        pl.when(self.takes)(lambda: self.copy.wait_recv())


def densify(get, rel, edge, put):
    weight = [jnp.where(rel[e] == edge, 1.0, 0.0).astype(jnp.float32) for e in range(E7)]

    def strip(i, carry):
        rows = pl.ds(pl.multiple_of(i * 64, 64), 64)
        blocks = [get(e, rows) for e in range(E7)]
        shared = blocks[0].astype(jnp.float32) * weight[0]
        for e in range(1, E7):
            shared = shared + blocks[e].astype(jnp.float32) * weight[e]
        shared = shared.astype(jnp.bfloat16)
        for k in range(10):
            block = jnp.where(edge == k, shared, jnp.zeros_like(shared))
            for e in range(E7):
                block = jnp.where((rel[e] == k) & (edge != k), blocks[e], block)
            put(i * 64, k, block)
        return carry

    lax.fori_loop(0, BS // 64, strip, 0)


def kernel(
    p, f, cols, taper, mask, noise, out,
    pown, up, dn, inter, fown, fbuf, drow, dcol, tap,
    hs, hr, zs, zr, s1, r1, s2, r2, s3, r3, lp, lf, lt,
):
    r, c = lax.axis_index("row"), lax.axis_index("col")
    x, y, z, k = r % 4, r // 4, c // 2, c % 2

    def dev(x, y, z, k):
        return (y * 4 + x, z * 2 + k)

    def chunk(s):
        return s + k * (3 - 2 * s)

    def lanes(ch):
        return pl.ds(pl.multiple_of(ch * CW, CW), CW)

    nxt, prv = ((r + 1) % 16, c), ((r + 15) % 16, c)
    zn, zp = (r, (c + 1) % 8), (r, (c + 7) % 8)
    X = [dev((x + d) % 4, y, z, k) for d in range(4)]
    Y = [dev(x, (y + d) % 4, z, k) for d in range(4)]

    load_f = pltpu.make_async_copy(f, fown, lf.at[0])
    load_p = [pltpu.make_async_copy(p.at[:, lanes(chunk(s))], pown.at[s], lp.at[s]) for s in range(4)]
    load_t = pltpu.make_async_copy(taper, tap, lt.at[0])
    load_f.start()
    for s in range(4):
        load_p[s].start()

    @pl.when(r == 0)
    def _():
        up[...] = jnp.zeros_like(up)

    @pl.when(r == 15)
    def _():
        dn[...] = jnp.zeros_like(dn)

    barrier = pltpu.get_barrier_semaphore()
    partners = [nxt, prv, zn, zp] + X[1:] + Y[1:]
    for t in partners:
        pl.semaphore_signal(barrier, inc=1, device_id=t, device_id_type=MESH)
    load_f.wait()

    def own_row(i, carry):
        pair, v = i // 2, i % 2
        base = r * 4 + 2 * pair - 4
        rel = [cols[e, r * 4 + i] - base for e in range(E7)]

        def put(row, kk, block):
            rows = pl.ds(pl.multiple_of(v * BS + row, 64), 64)
            drow[pair, rows, kk * BS:(kk + 1) * BS] = block

        densify(lambda e, rows: fown[i, e, rows, :], rel, jnp.where(r < 8, 0, 63) - base, put)
        return carry

    lax.fori_loop(0, 4, own_row, 0)

    pl.semaphore_wait(barrier, len(partners))

    source = x // 2 == k
    root = (y == z) & source
    h = x % 2

    def scatter(d, u):
        q = (y + d) % 4
        return remote(f.at[q, PART[u]], fbuf.at[q, h, PART[u]], s1.at[d, u], r1.at[u], Y[d])

    def along_x(d, g, u):
        here = fbuf.at[y, g, PART[u]]
        return remote(here, here, s2.at[d, u], r2.at[g, u], X[d])

    def along_y(d, g, u, to):
        here = fbuf.at[(y + 4 - d) % 4, g, PART[u]]
        there = (d + to) % 4
        return remote(here, here, s3.at[there, g, u], r3.at[there, g, u], Y[to % 4])

    def from_y(d, g, u):
        here = fbuf.at[(y + 4 - d) % 4, g, PART[u]]
        return remote(here, here, s3.at[0, 0, u], r3.at[d, g, u], Y[1])

    halo = []
    for s in range(4):
        piece = p.at[:, lanes(chunk(s))]
        halo.append((
            Between(remote(piece, up.at[s], hs.at[0, s], hr.at[0, s], nxt), r < 15, r > 0),
            Between(remote(piece, dn.at[s], hs.at[1, s], hr.at[1, s], prv), r > 0, r < 15),
        ))

    @pl.when(root)
    def _():
        for u in U:
            for d in (2, 1, 3):
                scatter(d, u).start()
        own = pltpu.make_async_copy(f.at[y], fbuf.at[y, h], lf.at[1])
        own.start()
        own.wait()

    held = (y == z) & (x == 3), (y == z) & (x == 0)
    for way in (0, 1):
        @pl.when(jnp.logical_not(held[way]))
        def _():
            halo[0][way].start()

    kinds = (x == 0, -1), (x == 3, 1)
    plain = (x == 1) | (x == 2)

    def send_y(g, u):
        @pl.when(plain)
        def _():
            for to in (1, -1):
                along_y(0, g, u, to).start()

        for cond, to in kinds:
            @pl.when(cond)
            def _():
                along_y(0, g, u, to).start()
                if g == 0:
                    along_y(0, g, u, -to).start()

    for u in U:
        @pl.when(source & (y != z))
        def _():
            scatter(1, u).wait_recv()

        @pl.when(source)
        def _():
            for d in (2, 1, 3):
                along_x(d, h, u).start()

        for g in (0, 1):
            @pl.when(x == 2 * k + g)
            def _():
                send_y(g, u)

    for u in U:
        for g in (0, 1):
            @pl.when(x != 2 * k + g)
            def _():
                along_x(1, g, u).wait_recv()
                send_y(g, u)

        if u == 1:
            for way in (0, 1):
                @pl.when(held[way])
                def _():
                    halo[0][way].start()

    for s in (1, 2, 3):
        for cp in halo[s]:
            cp.start()
    load_t.start()

    def col_rows(d, groups=(0, 2)):
        q = (y + 4 - d) % 4

        def one(g, carry):
            pair, v = 2 * g + q // 2, q % 2
            base = c * 8 + 2 * pair - 4
            rel = [cols[e, c * 8 + 4 * g + q] - base for e in range(E7)]

            def put(row, kk, block):
                rows = pl.ds(pl.multiple_of(v * BS + row, 64), 64)
                dcol[pair, kk // 2, rows, kk % 2 * BS:(kk % 2 + 1) * BS] = block

            densify(lambda e, rows: fbuf[q, g, e, rows, :], rel, jnp.where(c < 4, 0, 63) - base, put)
            return carry

        lax.fori_loop(*groups, one, 0)

    def first_product(s):
        for cp in halo[s]:
            cp.wait_recv()
        load_p[s].wait()
        ch = chunk(s)
        mid = pown[s]
        top = jnp.dot(drow[0, :, 0:512], up[s], preferred_element_type=jnp.float32)
        top += jnp.dot(drow[0, :, 512:1024], mid, preferred_element_type=jnp.float32)
        top += jnp.dot(drow[0, :, 1024:1280], dn[s, 0:256], preferred_element_type=jnp.float32)
        inter[ch + 2, 0:256] = top.astype(jnp.bfloat16)
        low = jnp.dot(drow[1, :, 0:256], up[s, 256:512], preferred_element_type=jnp.float32)
        low += jnp.dot(drow[1, :, 256:768], mid, preferred_element_type=jnp.float32)
        low += jnp.dot(drow[1, :, 768:1280], dn[s], preferred_element_type=jnp.float32)
        inter[ch + 2, 256:512] = low.astype(jnp.bfloat16)

        @pl.when(ch < 2)
        def _():
            remote(inter.at[ch + 2], inter.at[ch + 6], zs.at[s], zr.at[ch + 2], zp).start()

        @pl.when(ch >= 2)
        def _():
            remote(inter.at[ch + 2], inter.at[ch - 2], zs.at[s], zr.at[ch - 2], zn).start()

    first_product(0)
    col_rows(0)

    @pl.when(plain)
    def _():
        for u in U:
            from_y(1, 0, u).wait_recv()
            along_y(1, 0, u, 1).start()
            from_y(3, 1, u).wait_recv()
            along_y(3, 1, u, -1).start()

    for cond, to in kinds:
        @pl.when(cond)
        def _():
            for u in U:
                for g in (1, 0):
                    from_y(to % 4, g, u).wait_recv()
                    along_y(to % 4, g, u, to).start()

    first_product(1)

    @pl.when(plain)
    def _():
        for u in U:
            from_y(1, 1, u).wait_recv()

    first = jnp.where(x == 0, 3, 1)
    second = jnp.where(plain, 3, 2)
    third = jnp.where(plain, 2, jnp.where(x == 0, 1, 3))
    col_rows(first)

    for cond, to in kinds:
        @pl.when(cond)
        def _():
            for u in U:
                from_y(2, 1, u).wait_recv()
                along_y(2, 1, u, to).start()

    first_product(2)
    for u in U:
        from_y(second, 0, u).wait_recv()
    col_rows(second)

    def pair_of(i):
        return i + k * (3 - 2 * i)

    def chunk_of(e):
        return e + k * (7 - 2 * e)

    def from_z(e):
        slot = chunk_of(e)
        remote(
            inter.at[2], inter.at[slot], zs.at[0], zr.at[jnp.where(slot < 2, slot, slot - 4)], zn
        ).wait_recv()

    def products(i, chunks):
        ch = pair_of(i)
        total = None
        for e in chunks:
            slot = chunk_of(e)
            term = lax.dot_general(inter[slot], dcol[ch, slot - ch], NT, preferred_element_type=jnp.float32)
            total = term if total is None else total + term
        return total

    def begin(i):
        out[:, lanes(pair_of(i))] = products(i, READY[i])

    def finish(i, whole):
        ch = pair_of(i)
        if whole:
            spread = products(i, READY[i] + LAST[i])
        else:
            spread = out[:, lanes(ch)]
            if LAST[i]:
                spread = spread + products(i, LAST[i])
        lane = lax.broadcasted_iota(jnp.int32, (1, CW), 1)
        for v in range(4):
            rows = slice(v * BS, (v + 1) * BS)
            keep = jnp.where(
                lane < BS,
                mask[v, 2 * ch].astype(jnp.float32),
                mask[v, 2 * ch + 1].astype(jnp.float32),
            )
            out[rows, lanes(ch)] = spread[rows] * (tap[rows, lanes(ch)].astype(jnp.float32) * keep)
        for t in range(2):
            v = c * 8 + 2 * ch + t - r * 4

            @pl.when((v >= 0) & (v < 4))
            def _():
                eye = lax.broadcasted_iota(jnp.int32, (BS, BS), 0) == lax.broadcasted_iota(
                    jnp.int32, (BS, BS), 1
                )
                here = (
                    pl.ds(pl.multiple_of(v * BS, BS), BS),
                    pl.ds(pl.multiple_of(ch * CW + t * BS, BS), BS),
                )
                out[here] = out[here] + jnp.where(eye, noise[pl.ds(v, 1), :], 0.0)

    def last_rows(g):
        for u in U:
            from_y(third, g, u).wait_recv()
        col_rows(third, (g, g + 1))

    late = ((y + 4 - third) % 4) // 2
    for e in (0, 1, 7):
        from_z(e)
    load_t.wait()

    @pl.when(plain)
    def _():
        last_rows(0)
        last_rows(1)

    for i in range(4):
        @pl.when(plain | (pair_of(i) % 2 != late))
        def _():
            begin(i)

    first_product(3)

    @pl.when(jnp.logical_not(plain))
    def _():
        last_rows(0)
        for i in range(4):
            @pl.when(pair_of(i) == late)
            def _():
                begin(i)

    from_z(6)
    for i in range(4):
        @pl.when(plain | (pair_of(i) != 2 + late))
        def _():
            finish(i, False)

    @pl.when(jnp.logical_not(plain))
    def _():
        last_rows(1)
        for i in range(4):
            @pl.when(pair_of(i) == 2 + late)
            def _():
                finish(i, True)

    for s in range(4):
        for cp in halo[s]:
            cp.wait_send()
        remote(inter.at[2], inter.at[0], zs.at[s], zr.at[0], zn).wait_send()
    for u in U:
        for g in (0, 1):
            for d in (1, 2, 3):
                here = fbuf.at[0, 0, PART[u]]
                remote(here, here, s3.at[d, g, u], r3.at[d, g, u], Y[1]).wait_send()

        @pl.when(root)
        def _():
            for d in (1, 2, 3):
                scatter(d, u).wait_send()

        @pl.when(source)
        def _():
            for d in (1, 2, 3):
                along_x(d, h, u).wait_send()


def on_device(p_cov, f_blocks, stencil_cols, localization_weights, block_mask, disturbance_variances):
    noise = disturbance_variances.reshape(4, BS)
    bf = jnp.bfloat16
    dma = pltpu.SemaphoreType.DMA
    hbm = pl.BlockSpec(memory_space=pltpu.HBM)
    vmem = pl.BlockSpec(memory_space=pltpu.VMEM)
    smem = pl.BlockSpec(memory_space=pltpu.SMEM)
    return pl.pallas_call(
        kernel,
        out_shape=pltpu.VMEM((512, 1024), jnp.float32),
        in_specs=[hbm, hbm, smem, hbm, smem, vmem],
        out_specs=vmem,
        scratch_shapes=[
            pltpu.VMEM((4, 512, CW), bf),
            pltpu.VMEM((4, 512, CW), bf),
            pltpu.VMEM((4, 512, CW), bf),
            pltpu.VMEM((8, 512, CW), bf),
            pltpu.VMEM((4, E7, BS, BS), bf),
            pltpu.VMEM((4, 2, E7, BS, BS), bf),
            pltpu.VMEM((2, 256, 1280), bf),
            pltpu.VMEM((4, 5, CW, CW), bf),
            pltpu.VMEM((512, 1024), bf),
            dma((2, 4)), dma((2, 4)), dma((4,)), dma((4,)),
            dma((4, 3)), dma((3,)), dma((4, 3)), dma((2, 3)), dma((4, 2, 3)), dma((4, 2, 3)),
            dma((4,)), dma((2,)), dma((1,)),
        ],
        compiler_params=pltpu.CompilerParams(
            collective_id=0, has_side_effects=True, vmem_limit_bytes=VMEM_MB * 2**20
        ),
    )(p_cov, f_blocks, stencil_cols.T, localization_weights, block_mask, noise)

def solution(mesh):
    placed = (
        P("row", "col"),
        P("row", None, None, None),
        P(),
        P("row", "col"),
        P("row", "col"),
        P("row"),
    )
    return jax.shard_map(
        on_device, mesh=mesh, in_specs=placed, out_specs=P("row", "col"), check_vma=False
    )
```

```python
import jax
import jax.numpy as jnp
from jax import lax
from jax.experimental import pallas as pl
from jax.experimental.pallas import tpu as pltpu
from jax.sharding import PartitionSpec as P

MESH = pl.DeviceIdType.MESH
VMEM_MB = 60
E7 = 7
BS = 128
CW = 256
PART = (pl.ds(0, 2), pl.ds(2, 2), pl.ds(4, 3))
U = range(3)
READY = (0, 1, 2, 3, 4), (1, 2, 3, 4), (2, 3, 4), (3, 4, 7)
LAST = (), (5,), (5, 6), (5, 6)
NT = (((1,), (1,)), ((), ()))


def remote(src, dst, send, recv, to):
    return pltpu.make_async_remote_copy(src, dst, send, recv, device_id=to, device_id_type=MESH)


class Between:
    def __init__(self, copy, sends, takes):
        self.copy, self.sends, self.takes = copy, sends, takes

    def start(self):
        pl.when(self.sends)(lambda: self.copy.start())

    def wait_send(self):
        pl.when(self.sends)(lambda: self.copy.wait_send())

    def wait_recv(self):
        pl.when(self.takes)(lambda: self.copy.wait_recv())


def densify(get, rel, edge, put):
    weight = [jnp.where(rel[e] == edge, 1.0, 0.0).astype(jnp.float32) for e in range(E7)]

    def strip(i, carry):
        rows = pl.ds(pl.multiple_of(i * 64, 64), 64)
        blocks = [get(e, rows) for e in range(E7)]
        shared = blocks[0].astype(jnp.float32) * weight[0]
        for e in range(1, E7):
            shared = shared + blocks[e].astype(jnp.float32) * weight[e]
        shared = shared.astype(jnp.bfloat16)
        for k in range(10):
            block = jnp.where(edge == k, shared, jnp.zeros_like(shared))
            for e in range(E7):
                block = jnp.where((rel[e] == k) & (edge != k), blocks[e], block)
            put(i * 64, k, block)
        return carry

    lax.fori_loop(0, BS // 64, strip, 0)


def kernel(
    p, f, cols, taper, mask, noise, out,
    pown, up, dn, inter, fown, fbuf, drow, dcol, tap,
    hs, hr, zs, zr, s1, r1, s2, r2, s3, r3, lp, lf, lt,
):
    r, c = lax.axis_index("row"), lax.axis_index("col")
    x, y, z, k = r % 4, r // 4, c // 2, c % 2

    def dev(x, y, z, k):
        return (y * 4 + x, z * 2 + k)

    def chunk(s):
        return s + k * (3 - 2 * s)

    def lanes(ch):
        return pl.ds(pl.multiple_of(ch * CW, CW), CW)

    nxt, prv = ((r + 1) % 16, c), ((r + 15) % 16, c)
    zn, zp = (r, (c + 1) % 8), (r, (c + 7) % 8)
    X = [dev((x + d) % 4, y, z, k) for d in range(4)]
    Y = [dev(x, (y + d) % 4, z, k) for d in range(4)]

    load_f = pltpu.make_async_copy(f, fown, lf.at[0])
    load_p = [pltpu.make_async_copy(p.at[:, lanes(chunk(s))], pown.at[s], lp.at[s]) for s in range(4)]
    load_t = pltpu.make_async_copy(taper, tap, lt.at[0])
    load_f.start()
    for s in range(4):
        load_p[s].start()

    @pl.when(r == 0)
    def _():
        up[...] = jnp.zeros_like(up)

    @pl.when(r == 15)
    def _():
        dn[...] = jnp.zeros_like(dn)

    barrier = pltpu.get_barrier_semaphore()
    partners = [nxt, prv, zn, zp] + X[1:] + Y[1:]
    for t in partners:
        pl.semaphore_signal(barrier, inc=1, device_id=t, device_id_type=MESH)
    load_f.wait()

    def own_row(i, carry):
        pair, v = i // 2, i % 2
        base = r * 4 + 2 * pair - 4
        rel = [cols[e, r * 4 + i] - base for e in range(E7)]

        def put(row, kk, block):
            rows = pl.ds(pl.multiple_of(v * BS + row, 64), 64)
            drow[pair, rows, kk * BS:(kk + 1) * BS] = block

        densify(lambda e, rows: fown[i, e, rows, :], rel, jnp.where(r < 8, 0, 63) - base, put)
        return carry

    lax.fori_loop(0, 4, own_row, 0)

    pl.semaphore_wait(barrier, len(partners))

    source = x // 2 == k
    root = (y == z) & source
    h = x % 2

    def scatter(d, u):
        q = (y + d) % 4
        return remote(f.at[q, PART[u]], fbuf.at[q, h, PART[u]], s1.at[d, u], r1.at[u], Y[d])

    def along_x(d, g, u):
        here = fbuf.at[y, g, PART[u]]
        return remote(here, here, s2.at[d, u], r2.at[g, u], X[d])

    def along_y(d, g, u, to):
        here = fbuf.at[(y + 4 - d) % 4, g, PART[u]]
        there = (d + to) % 4
        return remote(here, here, s3.at[there, g, u], r3.at[there, g, u], Y[to % 4])

    def from_y(d, g, u):
        here = fbuf.at[(y + 4 - d) % 4, g, PART[u]]
        return remote(here, here, s3.at[0, 0, u], r3.at[d, g, u], Y[1])

    halo = []
    for s in range(4):
        piece = p.at[:, lanes(chunk(s))]
        halo.append((
            Between(remote(piece, up.at[s], hs.at[0, s], hr.at[0, s], nxt), r < 15, r > 0),
            Between(remote(piece, dn.at[s], hs.at[1, s], hr.at[1, s], prv), r > 0, r < 15),
        ))

    @pl.when(root)
    def _():
        for u in U:
            for d in (2, 1, 3):
                scatter(d, u).start()
        own = pltpu.make_async_copy(f.at[y], fbuf.at[y, h], lf.at[1])
        own.start()
        own.wait()

    held = (y == z) & (x == 3) & (k == 0), (y == z) & (x == 0) & (k == 1)
    for way in (0, 1):
        @pl.when(jnp.logical_not(held[way]))
        def _():
            halo[0][way].start()

    kinds = (x == 0, -1), (x == 3, 1)
    plain = (x == 1) | (x == 2)

    def send_y(g, u):
        @pl.when(plain)
        def _():
            for to in (1, -1):
                along_y(0, g, u, to).start()

        for cond, to in kinds:
            @pl.when(cond)
            def _():
                along_y(0, g, u, to).start()
                if g == 0:
                    along_y(0, g, u, -to).start()

    for u in U:
        @pl.when(source & (y != z))
        def _():
            scatter(1, u).wait_recv()

        @pl.when(source)
        def _():
            for d in (2, 1, 3):
                along_x(d, h, u).start()

        for g in (0, 1):
            @pl.when(x == 2 * k + g)
            def _():
                send_y(g, u)

    for u in U:
        for g in (0, 1):
            @pl.when(x != 2 * k + g)
            def _():
                along_x(1, g, u).wait_recv()
                send_y(g, u)

        if u == 1:
            for way in (0, 1):
                @pl.when(held[way])
                def _():
                    halo[0][way].start()

    for s in (1, 2, 3):
        for cp in halo[s]:
            cp.start()
    load_t.start()

    def col_rows(d, groups=(0, 2)):
        q = (y + 4 - d) % 4

        def one(g, carry):
            pair, v = 2 * g + q // 2, q % 2
            base = c * 8 + 2 * pair - 4
            rel = [cols[e, c * 8 + 4 * g + q] - base for e in range(E7)]

            def put(row, kk, block):
                rows = pl.ds(pl.multiple_of(v * BS + row, 64), 64)
                dcol[pair, kk // 2, rows, kk % 2 * BS:(kk % 2 + 1) * BS] = block

            densify(lambda e, rows: fbuf[q, g, e, rows, :], rel, jnp.where(c < 4, 0, 63) - base, put)
            return carry

        lax.fori_loop(*groups, one, 0)

    def first_product(s):
        for cp in halo[s]:
            cp.wait_recv()
        load_p[s].wait()
        ch = chunk(s)
        mid = pown[s]
        top = jnp.dot(drow[0, :, 0:512], up[s], preferred_element_type=jnp.float32)
        top += jnp.dot(drow[0, :, 512:1024], mid, preferred_element_type=jnp.float32)
        top += jnp.dot(drow[0, :, 1024:1280], dn[s, 0:256], preferred_element_type=jnp.float32)
        inter[ch + 2, 0:256] = top.astype(jnp.bfloat16)
        low = jnp.dot(drow[1, :, 0:256], up[s, 256:512], preferred_element_type=jnp.float32)
        low += jnp.dot(drow[1, :, 256:768], mid, preferred_element_type=jnp.float32)
        low += jnp.dot(drow[1, :, 768:1280], dn[s], preferred_element_type=jnp.float32)
        inter[ch + 2, 256:512] = low.astype(jnp.bfloat16)

        @pl.when(ch < 2)
        def _():
            remote(inter.at[ch + 2], inter.at[ch + 6], zs.at[s], zr.at[ch + 2], zp).start()

        @pl.when(ch >= 2)
        def _():
            remote(inter.at[ch + 2], inter.at[ch - 2], zs.at[s], zr.at[ch - 2], zn).start()

    first_product(0)
    col_rows(0)

    @pl.when(plain)
    def _():
        for u in U:
            from_y(1, 0, u).wait_recv()
            along_y(1, 0, u, 1).start()
            from_y(3, 1, u).wait_recv()
            along_y(3, 1, u, -1).start()

    for cond, to in kinds:
        @pl.when(cond)
        def _():
            for u in U:
                for g in (1, 0):
                    from_y(to % 4, g, u).wait_recv()
                    along_y(to % 4, g, u, to).start()

    first_product(1)

    @pl.when(plain)
    def _():
        for u in U:
            from_y(1, 1, u).wait_recv()

    first = jnp.where(x == 0, 3, 1)
    second = jnp.where(plain, 3, 2)
    third = jnp.where(plain, 2, jnp.where(x == 0, 1, 3))
    col_rows(first)

    for cond, to in kinds:
        @pl.when(cond)
        def _():
            for u in U:
                from_y(2, 1, u).wait_recv()
                along_y(2, 1, u, to).start()

    first_product(2)
    for u in U:
        from_y(second, 0, u).wait_recv()
    col_rows(second)

    def pair_of(i):
        return i + k * (3 - 2 * i)

    def chunk_of(e):
        return e + k * (7 - 2 * e)

    def from_z(e):
        slot = chunk_of(e)
        remote(
            inter.at[2], inter.at[slot], zs.at[0], zr.at[jnp.where(slot < 2, slot, slot - 4)], zn
        ).wait_recv()

    def products(i, chunks):
        ch = pair_of(i)
        total = None
        for e in chunks:
            slot = chunk_of(e)
            term = lax.dot_general(inter[slot], dcol[ch, slot - ch], NT, preferred_element_type=jnp.float32)
            total = term if total is None else total + term
        return total

    def begin(i):
        out[:, lanes(pair_of(i))] = products(i, READY[i])

    def finish(i, whole):
        ch = pair_of(i)
        if whole:
            spread = products(i, READY[i] + LAST[i])
        else:
            spread = out[:, lanes(ch)]
            if LAST[i]:
                spread = spread + products(i, LAST[i])
        lane = lax.broadcasted_iota(jnp.int32, (1, CW), 1)
        for v in range(4):
            rows = slice(v * BS, (v + 1) * BS)
            keep = jnp.where(
                lane < BS,
                mask[v, 2 * ch].astype(jnp.float32),
                mask[v, 2 * ch + 1].astype(jnp.float32),
            )
            out[rows, lanes(ch)] = spread[rows] * (tap[rows, lanes(ch)].astype(jnp.float32) * keep)
        for t in range(2):
            v = c * 8 + 2 * ch + t - r * 4

            @pl.when((v >= 0) & (v < 4))
            def _():
                eye = lax.broadcasted_iota(jnp.int32, (BS, BS), 0) == lax.broadcasted_iota(
                    jnp.int32, (BS, BS), 1
                )
                here = (
                    pl.ds(pl.multiple_of(v * BS, BS), BS),
                    pl.ds(pl.multiple_of(ch * CW + t * BS, BS), BS),
                )
                out[here] = out[here] + jnp.where(eye, noise[pl.ds(v, 1), :], 0.0)

    def last_rows(g):
        for u in U:
            from_y(third, g, u).wait_recv()
        col_rows(third, (g, g + 1))

    late = ((y + 4 - third) % 4) // 2
    for e in (0, 1, 7):
        from_z(e)
    load_t.wait()

    @pl.when(plain)
    def _():
        last_rows(0)
        last_rows(1)

    for i in range(4):
        @pl.when(plain | (pair_of(i) % 2 != late))
        def _():
            begin(i)

    first_product(3)

    @pl.when(jnp.logical_not(plain))
    def _():
        last_rows(0)
        for i in range(4):
            @pl.when(pair_of(i) == late)
            def _():
                begin(i)

    from_z(6)
    for i in range(4):
        @pl.when(plain | (pair_of(i) != 2 + late))
        def _():
            finish(i, False)

    @pl.when(jnp.logical_not(plain))
    def _():
        last_rows(1)
        for i in range(4):
            @pl.when(pair_of(i) == 2 + late)
            def _():
                finish(i, True)

    for s in range(4):
        for cp in halo[s]:
            cp.wait_send()
        remote(inter.at[2], inter.at[0], zs.at[s], zr.at[0], zn).wait_send()
    for u in U:
        for g in (0, 1):
            for d in (1, 2, 3):
                here = fbuf.at[0, 0, PART[u]]
                remote(here, here, s3.at[d, g, u], r3.at[d, g, u], Y[1]).wait_send()

        @pl.when(root)
        def _():
            for d in (1, 2, 3):
                scatter(d, u).wait_send()

        @pl.when(source)
        def _():
            for d in (1, 2, 3):
                along_x(d, h, u).wait_send()


def on_device(p_cov, f_blocks, stencil_cols, localization_weights, block_mask, disturbance_variances):
    noise = disturbance_variances.reshape(4, BS)
    bf = jnp.bfloat16
    dma = pltpu.SemaphoreType.DMA
    hbm = pl.BlockSpec(memory_space=pltpu.HBM)
    vmem = pl.BlockSpec(memory_space=pltpu.VMEM)
    smem = pl.BlockSpec(memory_space=pltpu.SMEM)
    return pl.pallas_call(
        kernel,
        out_shape=pltpu.VMEM((512, 1024), jnp.float32),
        in_specs=[hbm, hbm, smem, hbm, smem, vmem],
        out_specs=vmem,
        scratch_shapes=[
            pltpu.VMEM((4, 512, CW), bf),
            pltpu.VMEM((4, 512, CW), bf),
            pltpu.VMEM((4, 512, CW), bf),
            pltpu.VMEM((8, 512, CW), bf),
            pltpu.VMEM((4, E7, BS, BS), bf),
            pltpu.VMEM((4, 2, E7, BS, BS), bf),
            pltpu.VMEM((2, 256, 1280), bf),
            pltpu.VMEM((4, 5, CW, CW), bf),
            pltpu.VMEM((512, 1024), bf),
            dma((2, 4)), dma((2, 4)), dma((4,)), dma((4,)),
            dma((4, 3)), dma((3,)), dma((4, 3)), dma((2, 3)), dma((4, 2, 3)), dma((4, 2, 3)),
            dma((4,)), dma((2,)), dma((1,)),
        ],
        compiler_params=pltpu.CompilerParams(
            collective_id=0, has_side_effects=True, vmem_limit_bytes=VMEM_MB * 2**20
        ),
    )(p_cov, f_blocks, stencil_cols.T, localization_weights, block_mask, noise)

def solution(mesh):
    placed = (
        P("row", "col"),
        P("row", None, None, None),
        P(),
        P("row", "col"),
        P("row", "col"),
        P("row"),
    )
    return jax.shard_map(
        on_device, mesh=mesh, in_specs=placed, out_specs=P("row", "col"), check_vma=False
    )
```
